32 devices in a mesh: grp: 2 (over y), tok: 4 (over z), sec: 2 (over core), ch: 2 (over x).
Axes of the slice: x: 2, y: 2, z: 4, core: 2. Of those that a mesh axis runs over, the one named last changes fastest.
Arguments:
- features: bfloat16 [4096, 2048], P('ch', ('grp', 'tok', 'sec')), parts along dimension 1, may hold values from -6 to 6
- gate_one: bfloat16 [4096, 2048], P('ch', ('grp', 'tok', 'sec')), parts along dimension 1, may hold values from -6 to 6
- taps_one: bfloat16 [4096, 128], P('ch'), may hold values from -0.5 to 0.5
- long_filter: bfloat16 [4096, 1024], P('ch', ('tok', 'sec')), may hold values from -0.1875 to 0.1875
- skip_gain: float32 [4096], P('ch'), may hold values from 0.5 to 1.5
- taps_two: bfloat16 [4096, 128], P('ch'), may hold values from -0.5 to 0.5
- gate_two: bfloat16 [4096, 2048], P('ch', ('grp', 'tok', 'sec')), parts along dimension 1, may hold values from -6 to 6
Outputs:
- mixed_out: bfloat16 [4096, 2048], P('ch', ('grp', 'tok', 'sec')), parts along dimension 1
The draws below stay inside these ranges and needn't reach their ends.
There are 2 independent parts, one for each index of `grp`. The reference program is written for one: setup_inputs(seed, part) draws one part's arguments, and reference() takes and returns one part's arrays. A program takes and returns all parts, laid end to end along the dimension named above; an argument that names none is the same for every part. Nothing has to cross between parts.
All inputs are finite; a program needn't handle non-finite values.
Results may differ from the reference program's by a relative error of at most 0.0057.
Values may be sent and summed in bfloat16 or wider, within the bound.
A program may use at most 192 MiB of HBM per device.

```python
import jax
import jax.numpy as jnp
from jax import lax

D = 4096
TAPS = 128
SEQ = 1024


def block_scale(own_key, extent, cuts, smallest, top_value):
    level = 1.0
    for axis_at, blocks in cuts:
        draws = jax.random.uniform(jax.random.fold_in(jax.random.fold_in(own_key, 6), axis_at), (blocks,), jnp.float32, smallest / len(cuts), top_value / len(cuts))
        level = level * jnp.repeat(jnp.exp(draws), extent[axis_at] // blocks).reshape((-1,) + (1,) * (len(extent) - 1 - axis_at))
    return level


def centred(rng, dims, scale, bound, cuts=(), dtype=jnp.bfloat16):
    values = scale * jax.random.normal(rng, dims, jnp.float32)
    if cuts:
        values = values * block_scale(rng, dims, cuts, -0.22, 0.18)
    return jnp.clip(values, -bound, bound).astype(dtype)


def setup_inputs(seed: int = 0, part: int = 0) -> dict:
    key_of = jax.random.split(jax.random.key(seed), 8)
    part_splits = jax.random.split(jax.random.fold_in(key_of[7], part), 8)
    return {
        "features": centred(part_splits[0], (D, SEQ), 1.0, 6.0, ((0, 2), (1, 8))),
        "gate_one": centred(part_splits[1], (D, SEQ), 1.0, 6.0, ((0, 2), (1, 8))),
        "taps_one": centred(key_of[2], (D, TAPS), TAPS ** -0.5, 0.5, ((0, 2),)),
        "long_filter": centred(key_of[3], (D, SEQ), SEQ ** -0.5, 0.1875, ((0, 2), (1, 8))),
        "skip_gain": jnp.clip(0.5 + 1.0 * jax.random.uniform(key_of[4], (D,), jnp.float32) ** block_scale(key_of[4], (D,), ((0, 2),), -0.2, 0.2), 0.5, 1.5),
        "taps_two": centred(key_of[5], (D, TAPS), TAPS ** -0.5, 0.5, ((0, 2),)),
        "gate_two": centred(part_splits[6], (D, SEQ), 1.0, 6.0, ((0, 2), (1, 8))),
    }


def causal_conv(signal, kernel_taps):
    padded = jnp.pad(signal.astype(jnp.float32), ((0, 0), (TAPS - 1, 0)))
    taps_wide = kernel_taps.astype(jnp.float32)
    length = signal.shape[1]

    def add_tap(step, total):
        offset = (TAPS - 1 - step).astype(jnp.int32)
        shifted = lax.dynamic_slice_in_dim(padded, offset, length, 1)
        weight = lax.dynamic_slice_in_dim(taps_wide, jnp.asarray(step).astype(jnp.int32), 1, 1)
        return total + weight * shifted

    return lax.fori_loop(0, TAPS, add_tap, jnp.zeros(signal.shape, jnp.float32))


def long_block(pieces):
    signal, filter_row, gain_row = pieces
    total = 2 * SEQ
    signal_wide = signal.astype(jnp.float32)
    spectrum = jnp.fft.rfft(signal_wide, n=total) * jnp.fft.rfft(filter_row.astype(jnp.float32), n=total)
    conv_out = jnp.fft.irfft(spectrum, n=total)[:, :SEQ]
    return (conv_out + gain_row[:, None] * signal_wide).astype(jnp.bfloat16)


def reference(features, gate_one, taps_one, long_filter, skip_gain, taps_two, gate_two):
    mixed_one = (causal_conv(features, taps_one) * gate_one.astype(jnp.float32)).astype(jnp.bfloat16)
    blocks = D // 256
    long_out = lax.map(long_block, (mixed_one.reshape(blocks, 256, SEQ), long_filter.reshape(blocks, 256, SEQ), skip_gain.reshape(blocks, 256))).reshape(D, SEQ)
    return (causal_conv(long_out, taps_two) * gate_two.astype(jnp.float32)).astype(jnp.bfloat16)
```

```python
import math

import jax
import jax.numpy as jnp
import ml_dtypes
import numpy as np
from jax import lax
from jax.sharding import PartitionSpec as P

RING = ("tok", "sec")
TABLE_LIMIT = 1 << 23


def angles(tokens, half):
    steps = (np.arange(tokens)[:, None] * (2 * np.arange(half)[None, :] + 1)) % (4 * half)
    return steps * (math.pi / (2 * half))


def two_pieces(table):
    high = table.astype(ml_dtypes.bfloat16)
    low = (table - high.astype(np.float64)).astype(ml_dtypes.bfloat16)
    return high, low


def forward_table(tokens, half):
    angle = angles(tokens, half)
    return two_pieces(np.concatenate([np.cos(angle), -np.sin(angle)], axis=1))


def backward_table(tokens, half):
    angle = angles(tokens, half).T
    return two_pieces(np.concatenate([np.cos(angle), -np.sin(angle)], axis=0) / half)


def dot(left, right):
    return jnp.dot(left, right, preferred_element_type=jnp.float32)


def forward(signal, table):
    return dot(signal, table[0]) + dot(signal, table[1])


def backward(spectrum, table):
    high = spectrum.astype(jnp.bfloat16)
    low = (spectrum - high.astype(jnp.float32)).astype(jnp.bfloat16)
    return dot(high, table[0]) + dot(low, table[0]) + dot(high, table[1])


def times(left, right):
    half = left.shape[1] // 2
    a, b = left[:, :half], left[:, half:]
    c, d = right[:, :half], right[:, half:]
    return jnp.concatenate([a * c - b * d, a * d + b * c], axis=1)


def short_conv(before, block, taps):
    length = taps.shape[1]
    table = forward_table(2 * length, length)
    back = backward_table(2 * length, length)
    early = tuple(piece[:length] for piece in table)
    late = tuple(piece[length:] for piece in table)
    spectrum = forward(before, early) + forward(block, late)
    product = times(spectrum, forward(taps, early))
    return backward(product, tuple(piece[:, length:] for piece in back))


def angle_table(rows_count, cols_count, period):
    row_index = jnp.arange(rows_count, dtype=jnp.int32)[:, None]
    col_index = jnp.arange(cols_count, dtype=jnp.int32)[None, :]
    phase = (row_index * col_index % period).astype(jnp.float32) * (2.0 * math.pi / period)
    return (jnp.cos(phase), jnp.sin(phase))


def contract(form, left, right):
    return jnp.einsum(form, left, right, precision=lax.Precision.HIGHEST)


def forward_spectrum(signal, outer, inner, total):
    half_outer = outer // 2
    cos_first, sin_first = angle_table(half_outer, outer, outer)
    turn_cos, turn_sin = angle_table(outer, inner, total)
    cos_inner, sin_inner = angle_table(inner, inner, inner)
    shaped = signal.reshape(signal.shape[0], half_outer, inner)
    real_a = contract("cmn,mk->ckn", shaped, cos_first)
    imag_a = -contract("cmn,mk->ckn", shaped, sin_first)
    real_b = real_a * turn_cos + imag_a * turn_sin
    imag_b = imag_a * turn_cos - real_a * turn_sin
    real_c = contract("ckn,nj->cjk", real_b, cos_inner) + contract("ckn,nj->cjk", imag_b, sin_inner)
    imag_c = contract("ckn,nj->cjk", imag_b, cos_inner) - contract("ckn,nj->cjk", real_b, sin_inner)
    return (real_c, imag_c)


def inverse_spectrum(real_y, imag_y, outer, inner, total):
    half_outer = outer // 2
    cos_inner, sin_inner = angle_table(inner, inner, inner)
    turn_cos, turn_sin = angle_table(outer, inner, total)
    cos_last, sin_last = angle_table(outer, half_outer, outer)
    real_c = contract("cjk,jn->ckn", real_y, cos_inner) - contract("cjk,jn->ckn", imag_y, sin_inner)
    imag_c = contract("cjk,jn->ckn", imag_y, cos_inner) + contract("cjk,jn->ckn", real_y, sin_inner)
    real_d = real_c * turn_cos - imag_c * turn_sin
    imag_d = imag_c * turn_cos + real_c * turn_sin
    result = contract("ckn,km->cmn", real_d, cos_last) - contract("ckn,km->cmn", imag_d, sin_last)
    return (result / total).reshape(real_y.shape[0], half_outer * inner)


def factored_pair(signal, filter_rows, skip, taps):
    channels, seq_len = signal.shape
    length = taps.shape[1]
    total = 2 * seq_len
    inner = math.gcd(seq_len, 128)
    outer = total // inner
    wide = signal.astype(jnp.float32)
    a, b = forward_spectrum(wide, outer, inner, total)
    c, d = forward_spectrum(filter_rows.astype(jnp.float32), outer, inner, total)
    rows = inverse_spectrum(a * c - b * d, a * d + b * c, outer, inner, total) + skip * wide
    rows = rows.astype(jnp.bfloat16)
    blocks = seq_len // length
    before = jnp.pad(rows, ((0, 0), (length, 0)))[:, :seq_len]
    result = short_conv(
        before.reshape(channels * blocks, length),
        rows.reshape(channels * blocks, length),
        jnp.repeat(taps, blocks, axis=0),
    )
    return result.reshape(channels, seq_len)


def dense_pair(signal, filter_rows, skip, taps, half):
    seq_len = signal.shape[1]
    table = forward_table(seq_len, half)
    weights = forward(filter_rows, table)
    weights = jnp.concatenate([weights[:, :half] + skip, weights[:, half:]], axis=1)
    weights = times(weights, forward(taps, tuple(piece[: taps.shape[1]] for piece in table)))
    return backward(times(forward(signal, table), weights), backward_table(seq_len, half))


def exchange(blocks):
    return lax.all_to_all(blocks, RING, split_axis=0, concat_axis=0, tiled=True)


def on_device(features, gate_one, taps_one, long_filter, skip_gain, taps_two, gate_two):
    shards = lax.axis_size(RING)
    channels, block_len = features.shape
    narrow = channels // shards
    seq_len = block_len * shards
    length = taps_one.shape[1]

    def rows_of(blocks):
        return jnp.swapaxes(blocks, 0, 1).reshape(narrow, seq_len)

    filter_rows = rows_of(exchange(long_filter.reshape(shards, narrow, block_len)))
    before = lax.ppermute(features, RING, [(i, i + 1) for i in range(shards - 1)])
    mixed_one = (short_conv(before, features, taps_one) * gate_one).astype(jnp.bfloat16)
    signal = rows_of(exchange(mixed_one.reshape(shards, narrow, block_len)))
    first = lax.axis_index(RING) * narrow
    skip = lax.dynamic_slice_in_dim(skip_gain, first, narrow)[:, None]
    taps = lax.dynamic_slice_in_dim(taps_two, first, narrow)
    half = -(-(2 * seq_len + length) // 256) * 128
    if seq_len * half <= TABLE_LIMIT:
        result = dense_pair(signal, filter_rows, skip, taps, half)
    else:
        result = factored_pair(signal, filter_rows, skip, taps)
    result = result.astype(jnp.bfloat16).reshape(narrow, shards, block_len)
    second_conv = exchange(jnp.swapaxes(result, 0, 1)).reshape(channels, block_len)
    return (second_conv.astype(jnp.float32) * gate_two).astype(jnp.bfloat16)


def solution(mesh):
    in_specs = (
        P("ch", ("grp", "tok", "sec")),
        P("ch", ("grp", "tok", "sec")),
        P("ch", None),
        P("ch", ("tok", "sec")),
        P("ch"),
        P("ch", None),
        P("ch", ("grp", "tok", "sec")),
    )
    out_specs = P("ch", ("grp", "tok", "sec"))
    return jax.shard_map(
        on_device, mesh=mesh, in_specs=in_specs, out_specs=out_specs, check_vma=False
    )
```

```python
import math

import jax
import jax.numpy as jnp
import ml_dtypes
import numpy as np
from jax import lax
from jax.experimental import pallas as pl
from jax.experimental.pallas import tpu as pltpu
from jax.sharding import PartitionSpec as P

RING = ("tok", "sec")
TABLE_LIMIT = 1 << 23


def angles(tokens, half):
    steps = (np.arange(tokens)[:, None] * (2 * np.arange(half)[None, :] + 1)) % (4 * half)
    return steps * (math.pi / (2 * half))


def two_pieces(table):
    high = table.astype(ml_dtypes.bfloat16)
    low = (table - high.astype(np.float64)).astype(ml_dtypes.bfloat16)
    return high, low


def forward_table(tokens, half):
    angle = angles(tokens, half)
    return two_pieces(np.concatenate([np.cos(angle), -np.sin(angle)], axis=1))


def backward_table(tokens, half):
    angle = angles(tokens, half).T
    return two_pieces(np.concatenate([np.cos(angle), -np.sin(angle)], axis=0) / half)


def dot(left, right):
    return jnp.dot(left, right, preferred_element_type=jnp.float32)


def forward(signal, table):
    return dot(signal, table[0]) + dot(signal, table[1])


def backward(spectrum, table):
    high = spectrum.astype(jnp.bfloat16)
    low = (spectrum - high.astype(jnp.float32)).astype(jnp.bfloat16)
    return dot(high, table[0]) + dot(low, table[0]) + dot(high, table[1])


def times(left, right):
    half = left.shape[1] // 2
    a, b = left[:, :half], left[:, half:]
    c, d = right[:, :half], right[:, half:]
    return jnp.concatenate([a * c - b * d, a * d + b * c], axis=1)


def short_conv(before, block, taps):
    length = taps.shape[1]
    table = forward_table(2 * length, length)
    back = backward_table(2 * length, length)
    early = tuple(piece[:length] for piece in table)
    late = tuple(piece[length:] for piece in table)
    spectrum = forward(before, early) + forward(block, late)
    product = times(spectrum, forward(taps, early))
    return backward(product, tuple(piece[:, length:] for piece in back))


def angle_table(rows_count, cols_count, period):
    row_index = jnp.arange(rows_count, dtype=jnp.int32)[:, None]
    col_index = jnp.arange(cols_count, dtype=jnp.int32)[None, :]
    phase = (row_index * col_index % period).astype(jnp.float32) * (2.0 * math.pi / period)
    return (jnp.cos(phase), jnp.sin(phase))


def contract(form, left, right):
    return jnp.einsum(form, left, right, precision=lax.Precision.HIGHEST)


def forward_spectrum(signal, outer, inner, total):
    half_outer = outer // 2
    cos_first, sin_first = angle_table(half_outer, outer, outer)
    turn_cos, turn_sin = angle_table(outer, inner, total)
    cos_inner, sin_inner = angle_table(inner, inner, inner)
    shaped = signal.reshape(signal.shape[0], half_outer, inner)
    real_a = contract("cmn,mk->ckn", shaped, cos_first)
    imag_a = -contract("cmn,mk->ckn", shaped, sin_first)
    real_b = real_a * turn_cos + imag_a * turn_sin
    imag_b = imag_a * turn_cos - real_a * turn_sin
    real_c = contract("ckn,nj->cjk", real_b, cos_inner) + contract("ckn,nj->cjk", imag_b, sin_inner)
    imag_c = contract("ckn,nj->cjk", imag_b, cos_inner) - contract("ckn,nj->cjk", real_b, sin_inner)
    return (real_c, imag_c)


def inverse_spectrum(real_y, imag_y, outer, inner, total):
    half_outer = outer // 2
    cos_inner, sin_inner = angle_table(inner, inner, inner)
    turn_cos, turn_sin = angle_table(outer, inner, total)
    cos_last, sin_last = angle_table(outer, half_outer, outer)
    real_c = contract("cjk,jn->ckn", real_y, cos_inner) - contract("cjk,jn->ckn", imag_y, sin_inner)
    imag_c = contract("cjk,jn->ckn", imag_y, cos_inner) + contract("cjk,jn->ckn", real_y, sin_inner)
    real_d = real_c * turn_cos - imag_c * turn_sin
    imag_d = imag_c * turn_cos + real_c * turn_sin
    result = contract("ckn,km->cmn", real_d, cos_last) - contract("ckn,km->cmn", imag_d, sin_last)
    return (result / total).reshape(real_y.shape[0], half_outer * inner)


def factored_pair(signal, filter_rows, skip, taps):
    channels, seq_len = signal.shape
    length = taps.shape[1]
    total = 2 * seq_len
    inner = math.gcd(seq_len, 128)
    outer = total // inner
    wide = signal.astype(jnp.float32)
    a, b = forward_spectrum(wide, outer, inner, total)
    c, d = forward_spectrum(filter_rows.astype(jnp.float32), outer, inner, total)
    rows = inverse_spectrum(a * c - b * d, a * d + b * c, outer, inner, total) + skip * wide
    rows = rows.astype(jnp.bfloat16)
    blocks = seq_len // length
    before = jnp.pad(rows, ((0, 0), (length, 0)))[:, :seq_len]
    result = short_conv(
        before.reshape(channels * blocks, length),
        rows.reshape(channels * blocks, length),
        jnp.repeat(taps, blocks, axis=0),
    )
    return result.reshape(channels, seq_len)


def tiled_table(tokens, half):
    angle = angles(tokens, half).reshape(tokens, half // 128, 1, 128)
    table = np.concatenate([np.cos(angle), -np.sin(angle)], axis=2)
    return two_pieces(table.reshape(tokens, 2 * half))


def dot_rows(left, right):
    return lax.dot_general(
        left, right, (((1,), (1,)), ((), ())), preferred_element_type=jnp.float32
    )


def split(wide):
    high = wide.astype(jnp.bfloat16)
    return high, (wide - high.astype(jnp.float32)).astype(jnp.bfloat16)


def fused_kernel(
    features, gate_one, taps_one, long_filter, taps_two, skip, short_high, short_low,
    table_hbm, table_low, second_conv,
    table, before, filter_rows, signal, mixed_send, result_send, weights, high, low,
    table_sem, halo_sems, filter_sent, filter_got, mixed_sent, mixed_got, result_sent, result_got,
):
    sections = lax.axis_size("sec")
    shards = lax.axis_size("tok") * sections
    me = lax.axis_index("tok") * sections + lax.axis_index("sec")
    narrow, seq_len = signal.shape
    length = features.shape[1]
    tiles = weights.shape[0]
    half = tiles * 128

    def place(peer):
        return {"tok": peer // sections, "sec": peer % sections}

    def rows(peer):
        return pl.ds(pl.multiple_of(peer * narrow, narrow), narrow)

    def tokens(peer):
        return pl.ds(pl.multiple_of(peer * length, length), length)

    def other(step):
        return lax.rem(me + step, shards)

    def remote(source, target, sent, got, peer):
        return pltpu.make_async_remote_copy(
            src_ref=source, dst_ref=target, send_sem=sent, recv_sem=got,
            device_id=place(peer), device_id_type=pl.DeviceIdType.MESH,
        )

    load = pltpu.make_async_copy(table_hbm, table, table_sem)
    load.start()
    barrier = pltpu.get_barrier_semaphore()
    for step in range(1, shards):
        pl.semaphore_signal(
            barrier, inc=1, device_id=place(other(step)), device_id_type=pl.DeviceIdType.MESH
        )
    pl.semaphore_wait(barrier, shards - 1)

    halo = remote(features, before, halo_sems.at[0], halo_sems.at[1], other(1))

    @pl.when(me < shards - 1)
    def _():
        halo.start()

    def filter_copy(peer, slot):
        return remote(
            long_filter.at[rows(peer)], filter_rows.at[:, tokens(slot)],
            filter_sent.at[peer], filter_got.at[slot], peer,
        )

    def mixed_copy(peer, slot):
        return remote(
            mixed_send.at[peer], signal.at[:, tokens(slot)],
            mixed_sent.at[peer], mixed_got.at[slot], peer,
        )

    def result_copy(peer, slot):
        return remote(
            result_send.at[peer], second_conv.at[rows(slot)],
            result_sent.at[peer], result_got.at[slot], peer,
        )

    for step in range(1, shards):
        filter_copy(other(step), me).start()
    filter_rows[:, tokens(me)] = long_filter[rows(me)]

    @pl.when(me == 0)
    def _():
        before[...] = jnp.zeros_like(before)

    @pl.when(me > 0)
    def _():
        halo.wait_recv()

    early = (short_high[:length], short_low[:length])
    late = (short_high[length:], short_low[length:])

    def first_conv(peer):
        part = rows(peer)
        spectrum = forward(before[part], early) + forward(features[part], late)
        x_high, x_low = split(times(spectrum, forward(taps_one[part], early)))
        conv = dot_rows(x_high, late[0]) + dot_rows(x_low, late[0]) + dot_rows(x_high, late[1])
        return (conv * (1.0 / length) * gate_one[part].astype(jnp.float32)).astype(jnp.bfloat16)

    @pl.loop(1, shards)
    def _(step):
        peer = other(step)
        mixed_send[peer] = first_conv(peer)
        mixed_copy(peer, me).start()

    signal[:, tokens(me)] = first_conv(me)

    load.wait()
    for step in range(1, shards):
        filter_copy(other(step), other(step)).wait_recv()

    def columns(tile):
        return pl.ds(pl.multiple_of(tile * 256, 256), 256)

    gain = skip[...]
    taps = taps_two[rows(me)]

    @pl.loop(0, tiles)
    def _(tile):
        own = columns(tile)
        spectrum = dot(filter_rows[...], table[:, own])
        spectrum = jnp.concatenate([spectrum[:, :128] + gain, spectrum[:, 128:]], axis=1)
        short = dot(taps, table[:length, own]) + dot(taps, table_low[:, own])
        weights[tile] = times(spectrum, short) * (1.0 / half)

    for step in range(1, shards):
        mixed_copy(other(step), other(step)).wait_recv()

    @pl.loop(0, tiles)
    def _(tile):
        own = columns(tile)
        x_high, x_low = split(times(dot(signal[...], table[:, own]), weights[tile]))
        high[:, own] = x_high
        low[:, own] = x_low

    width = sections * length
    groups = shards // sections

    @pl.loop(1, groups + 1)
    def _(step):
        group = lax.rem(lax.axis_index("tok") + step, groups)
        part = table[pl.ds(pl.multiple_of(group * width, width), width)]
        result = (dot_rows(high[...], part) + dot_rows(low[...], part)).astype(jnp.bfloat16)
        for section in range(sections):
            peer = group * sections + section
            block = result[:, section * length : (section + 1) * length]

            @pl.when(peer != me)
            def _():
                result_send[peer] = block
                result_copy(peer, me).start()

            @pl.when(peer == me)
            def _():
                second_conv[rows(me)] = block

    for step in range(1, shards):
        result_copy(other(step), other(step)).wait_recv()
    for step in range(1, shards):
        filter_copy(other(step), me).wait_send()
        mixed_copy(other(step), me).wait_send()
        result_copy(other(step), me).wait_send()

    @pl.when(me < shards - 1)
    def _():
        halo.wait_send()


def fused(features, gate_one, taps_one, long_filter, taps_two, skip, shards, half):
    channels, length = features.shape
    narrow = channels // shards
    seq_len = shards * length
    table, table_low = tiled_table(seq_len, half)
    short_high, short_low = forward_table(2 * length, length)
    vmem = pl.BlockSpec(memory_space=pltpu.VMEM)
    half_type = jnp.bfloat16
    peers = pltpu.SemaphoreType.DMA((shards,))
    return pl.pallas_call(
        fused_kernel,
        out_shape=jax.ShapeDtypeStruct((channels, length), half_type),
        in_specs=[vmem] * 8 + [pl.BlockSpec(memory_space=pl.ANY), vmem],
        out_specs=vmem,
        scratch_shapes=[
            pltpu.VMEM((seq_len, 2 * half), half_type),
            pltpu.VMEM((channels, length), half_type),
            pltpu.VMEM((narrow, seq_len), half_type),
            pltpu.VMEM((narrow, seq_len), half_type),
            pltpu.VMEM((shards, narrow, length), half_type),
            pltpu.VMEM((shards, narrow, length), half_type),
            pltpu.VMEM((half // 128, narrow, 256), jnp.float32),
            pltpu.VMEM((narrow, 2 * half), half_type),
            pltpu.VMEM((narrow, 2 * half), half_type),
            pltpu.SemaphoreType.DMA,
            pltpu.SemaphoreType.DMA((2,)),
            peers, peers, peers, peers, peers, peers,
        ],
        compiler_params=pltpu.CompilerParams(
            collective_id=0, has_side_effects=True, vmem_limit_bytes=40 * 1024 * 1024
        ),
    )(features, gate_one, taps_one, long_filter, taps_two, skip, short_high, short_low,
      table, table_low[:length])


def exchange(blocks):
    return lax.all_to_all(blocks, RING, split_axis=0, concat_axis=0, tiled=True)


def on_device(features, gate_one, taps_one, long_filter, skip_gain, taps_two, gate_two):
    shards = lax.axis_size(RING)
    channels, block_len = features.shape
    narrow = channels // shards
    seq_len = block_len * shards
    length = taps_one.shape[1]

    first = lax.axis_index(RING) * narrow
    skip = lax.dynamic_slice_in_dim(skip_gain, first, narrow)[:, None]
    half = -(-(2 * seq_len + length) // 256) * 128
    if seq_len * half <= TABLE_LIMIT:
        second_conv = fused(
            features, gate_one, taps_one, long_filter, taps_two, skip, shards, half
        )
        return (second_conv.astype(jnp.float32) * gate_two).astype(jnp.bfloat16)

    def rows_of(blocks):
        return jnp.swapaxes(blocks, 0, 1).reshape(narrow, seq_len)

    filter_rows = rows_of(exchange(long_filter.reshape(shards, narrow, block_len)))
    before = lax.ppermute(features, RING, [(i, i + 1) for i in range(shards - 1)])
    mixed_one = (short_conv(before, features, taps_one) * gate_one).astype(jnp.bfloat16)
    signal = rows_of(exchange(mixed_one.reshape(shards, narrow, block_len)))
    taps = lax.dynamic_slice_in_dim(taps_two, first, narrow)
    result = factored_pair(signal, filter_rows, skip, taps)
    result = result.astype(jnp.bfloat16).reshape(narrow, shards, block_len)
    second_conv = exchange(jnp.swapaxes(result, 0, 1)).reshape(channels, block_len)
    return (second_conv.astype(jnp.float32) * gate_two).astype(jnp.bfloat16)


def solution(mesh):
    in_specs = (
        P("ch", ("grp", "tok", "sec")),
        P("ch", ("grp", "tok", "sec")),
        P("ch", None),
        P("ch", ("tok", "sec")),
        P("ch"),
        P("ch", None),
        P("ch", ("grp", "tok", "sec")),
    )
    out_specs = P("ch", ("grp", "tok", "sec"))
    return jax.shard_map(
        on_device, mesh=mesh, in_specs=in_specs, out_specs=out_specs, check_vma=False
    )
```

```python
import math

import jax
import jax.numpy as jnp
import ml_dtypes
import numpy as np
from jax import lax
from jax.experimental import pallas as pl
from jax.experimental.pallas import tpu as pltpu
from jax.sharding import PartitionSpec as P

RING = ("tok", "sec")
TABLE_LIMIT = 1 << 23


def angles(tokens, half):
    steps = (np.arange(tokens)[:, None] * (2 * np.arange(half)[None, :] + 1)) % (4 * half)
    return steps * (math.pi / (2 * half))


def two_pieces(table):
    high = table.astype(ml_dtypes.bfloat16)
    low = (table - high.astype(np.float64)).astype(ml_dtypes.bfloat16)
    return high, low


def forward_table(tokens, half):
    angle = angles(tokens, half)
    return two_pieces(np.concatenate([np.cos(angle), -np.sin(angle)], axis=1))


def backward_table(tokens, half):
    angle = angles(tokens, half).T
    return two_pieces(np.concatenate([np.cos(angle), -np.sin(angle)], axis=0) / half)


def dot(left, right):
    return jnp.dot(left, right, preferred_element_type=jnp.float32)


def forward(signal, table):
    return dot(signal, table[0]) + dot(signal, table[1])


def backward(spectrum, table):
    high = spectrum.astype(jnp.bfloat16)
    low = (spectrum - high.astype(jnp.float32)).astype(jnp.bfloat16)
    return dot(high, table[0]) + dot(low, table[0]) + dot(high, table[1])


def times(left, right):
    half = left.shape[1] // 2
    a, b = left[:, :half], left[:, half:]
    c, d = right[:, :half], right[:, half:]
    return jnp.concatenate([a * c - b * d, a * d + b * c], axis=1)


def short_conv(before, block, taps):
    length = taps.shape[1]
    table = forward_table(2 * length, length)
    back = backward_table(2 * length, length)
    early = tuple(piece[:length] for piece in table)
    late = tuple(piece[length:] for piece in table)
    spectrum = forward(before, early) + forward(block, late)
    product = times(spectrum, forward(taps, early))
    return backward(product, tuple(piece[:, length:] for piece in back))


def angle_table(rows_count, cols_count, period):
    row_index = jnp.arange(rows_count, dtype=jnp.int32)[:, None]
    col_index = jnp.arange(cols_count, dtype=jnp.int32)[None, :]
    phase = (row_index * col_index % period).astype(jnp.float32) * (2.0 * math.pi / period)
    return (jnp.cos(phase), jnp.sin(phase))


def contract(form, left, right):
    return jnp.einsum(form, left, right, precision=lax.Precision.HIGHEST)


def forward_spectrum(signal, outer, inner, total):
    half_outer = outer // 2
    cos_first, sin_first = angle_table(half_outer, outer, outer)
    turn_cos, turn_sin = angle_table(outer, inner, total)
    cos_inner, sin_inner = angle_table(inner, inner, inner)
    shaped = signal.reshape(signal.shape[0], half_outer, inner)
    real_a = contract("cmn,mk->ckn", shaped, cos_first)
    imag_a = -contract("cmn,mk->ckn", shaped, sin_first)
    real_b = real_a * turn_cos + imag_a * turn_sin
    imag_b = imag_a * turn_cos - real_a * turn_sin
    real_c = contract("ckn,nj->cjk", real_b, cos_inner) + contract("ckn,nj->cjk", imag_b, sin_inner)
    imag_c = contract("ckn,nj->cjk", imag_b, cos_inner) - contract("ckn,nj->cjk", real_b, sin_inner)
    return (real_c, imag_c)


def inverse_spectrum(real_y, imag_y, outer, inner, total):
    half_outer = outer // 2
    cos_inner, sin_inner = angle_table(inner, inner, inner)
    turn_cos, turn_sin = angle_table(outer, inner, total)
    cos_last, sin_last = angle_table(outer, half_outer, outer)
    real_c = contract("cjk,jn->ckn", real_y, cos_inner) - contract("cjk,jn->ckn", imag_y, sin_inner)
    imag_c = contract("cjk,jn->ckn", imag_y, cos_inner) + contract("cjk,jn->ckn", real_y, sin_inner)
    real_d = real_c * turn_cos - imag_c * turn_sin
    imag_d = imag_c * turn_cos + real_c * turn_sin
    result = contract("ckn,km->cmn", real_d, cos_last) - contract("ckn,km->cmn", imag_d, sin_last)
    return (result / total).reshape(real_y.shape[0], half_outer * inner)


def factored_pair(signal, filter_rows, skip, taps):
    channels, seq_len = signal.shape
    length = taps.shape[1]
    total = 2 * seq_len
    inner = math.gcd(seq_len, 128)
    outer = total // inner
    wide = signal.astype(jnp.float32)
    a, b = forward_spectrum(wide, outer, inner, total)
    c, d = forward_spectrum(filter_rows.astype(jnp.float32), outer, inner, total)
    rows = inverse_spectrum(a * c - b * d, a * d + b * c, outer, inner, total) + skip * wide
    rows = rows.astype(jnp.bfloat16)
    blocks = seq_len // length
    before = jnp.pad(rows, ((0, 0), (length, 0)))[:, :seq_len]
    result = short_conv(
        before.reshape(channels * blocks, length),
        rows.reshape(channels * blocks, length),
        jnp.repeat(taps, blocks, axis=0),
    )
    return result.reshape(channels, seq_len)


def tiled_table(tokens, half):
    angle = angles(tokens, half).reshape(tokens, half // 128, 1, 128)
    table = np.concatenate([np.cos(angle), -np.sin(angle)], axis=2)
    return two_pieces(table.reshape(tokens, 2 * half))


def dot_rows(left, right):
    return lax.dot_general(
        left, right, (((1,), (1,)), ((), ())), preferred_element_type=jnp.float32
    )


def split(wide):
    high = wide.astype(jnp.bfloat16)
    return high, (wide - high.astype(jnp.float32)).astype(jnp.bfloat16)


def fused_kernel(
    features_hbm, gate_hbm, taps_hbm, long_filter, taps_two, short_high_hbm, short_low_hbm,
    table_hbm, table_low_hbm, skip, second_conv,
    features, gate_one, taps_one, own_taps, short_high, short_low, table_low,
    table, before, filter_rows, signal, mixed_send, result_send, weights, high,
    load_sems, halo_sems, filter_sent, filter_got, mixed_sent, mixed_got, result_sent, result_got,
):
    sections = lax.axis_size("sec")
    shards = lax.axis_size("tok") * sections
    me = lax.axis_index("tok") * sections + lax.axis_index("sec")
    narrow, seq_len = signal.shape
    length = features.shape[1]
    tiles = weights.shape[0]
    half = tiles * 128

    def place(peer):
        return {"tok": peer // sections, "sec": peer % sections}

    def rows(peer):
        return pl.ds(pl.multiple_of(peer * narrow, narrow), narrow)

    def tokens(peer):
        return pl.ds(pl.multiple_of(peer * length, length), length)

    def other(step):
        return lax.rem(me + step, shards)

    def remote(source, target, sent, got, peer):
        return pltpu.make_async_remote_copy(
            src_ref=source, dst_ref=target, send_sem=sent, recv_sem=got,
            device_id=place(peer), device_id_type=pl.DeviceIdType.MESH,
        )

    pairs = (
        (features_hbm, features), (taps_hbm, taps_one), (short_high_hbm, short_high),
        (short_low_hbm, short_low), (gate_hbm, gate_one),
        (long_filter.at[rows(me)], filter_rows.at[:, tokens(me)]),
        (taps_two.at[rows(me)], own_taps), (table_low_hbm, table_low), (table_hbm, table),
    )
    loads = [
        pltpu.make_async_copy(source, target, load_sems.at[index])
        for index, (source, target) in enumerate(pairs)
    ]
    for load in loads:
        load.start()
    barrier = pltpu.get_barrier_semaphore()
    for step in range(1, shards):
        pl.semaphore_signal(
            barrier, inc=1, device_id=place(other(step)), device_id_type=pl.DeviceIdType.MESH
        )
    pl.semaphore_wait(barrier, shards - 1)

    halo = remote(features_hbm, before, halo_sems.at[0], halo_sems.at[1], other(1))

    @pl.when(me < shards - 1)
    def _():
        halo.start()

    def filter_copy(peer, slot):
        return remote(
            long_filter.at[rows(peer)], filter_rows.at[:, tokens(slot)],
            filter_sent.at[peer], filter_got.at[slot], peer,
        )

    def mixed_copy(peer, slot):
        return remote(
            mixed_send.at[peer], signal.at[:, tokens(slot)],
            mixed_sent.at[peer], mixed_got.at[slot], peer,
        )

    def result_copy(peer, slot):
        return remote(
            result_send.at[peer], second_conv.at[rows(slot)],
            result_sent.at[peer], result_got.at[slot], peer,
        )

    for step in range(1, shards):
        filter_copy(other(step), me).start()

    @pl.when(me == 0)
    def _():
        before[...] = jnp.zeros_like(before)

    @pl.when(me > 0)
    def _():
        halo.wait_recv()

    for load in loads[:5]:
        load.wait()
    early = (short_high[:length], short_low[:length])
    late = (short_high[length:], short_low[length:])

    def first_conv(peer):
        part = rows(peer)
        spectrum = forward(before[part], early) + forward(features[part], late)
        x_high, x_low = split(times(spectrum, forward(taps_one[part], early)))
        conv = dot_rows(x_high, late[0]) + dot_rows(x_low, late[0]) + dot_rows(x_high, late[1])
        return (conv * (1.0 / length) * gate_one[part].astype(jnp.float32)).astype(jnp.bfloat16)

    @pl.loop(1, shards)
    def _(step):
        peer = other(step)
        mixed_send[peer] = first_conv(peer)
        mixed_copy(peer, me).start()

    signal[:, tokens(me)] = first_conv(me)

    for load in loads[5:]:
        load.wait()
    for step in range(1, shards):
        filter_copy(other(step), other(step)).wait_recv()

    def columns(tile):
        return pl.ds(pl.multiple_of(tile * 256, 256), 256)

    gain = skip[...]
    taps = own_taps[...]

    @pl.loop(0, tiles)
    def _(tile):
        own = columns(tile)
        spectrum = dot(filter_rows[...], table[:, own])
        spectrum = jnp.concatenate([spectrum[:, :128] + gain, spectrum[:, 128:]], axis=1)
        short = dot(taps, table[:length, own]) + dot(taps, table_low[:, own])
        weights[tile] = times(spectrum, short) * (1.0 / half)

    for step in range(1, shards):
        mixed_copy(other(step), other(step)).wait_recv()

    @pl.loop(0, tiles)
    def _(tile):
        own = columns(tile)
        product = times(dot(signal[...], table[:, own]), weights[tile])
        high[:, own] = product.astype(jnp.bfloat16)

    width = sections * length
    groups = shards // sections

    @pl.loop(1, groups + 1)
    def _(step):
        group = lax.rem(lax.axis_index("tok") + step, groups)
        part = table[pl.ds(pl.multiple_of(group * width, width), width)]
        result = dot_rows(high[...], part).astype(jnp.bfloat16)
        for section in range(sections):
            peer = group * sections + section
            block = result[:, section * length : (section + 1) * length]

            @pl.when(peer != me)
            def _():
                result_send[peer] = block
                result_copy(peer, me).start()

            @pl.when(peer == me)
            def _():
                second_conv[rows(me)] = block

    for step in range(1, shards):
        result_copy(other(step), other(step)).wait_recv()
    for step in range(1, shards):
        filter_copy(other(step), me).wait_send()
        mixed_copy(other(step), me).wait_send()
        result_copy(other(step), me).wait_send()

    @pl.when(me < shards - 1)
    def _():
        halo.wait_send()


def fused(features, gate_one, taps_one, long_filter, taps_two, skip, shards, half):
    channels, length = features.shape
    narrow = channels // shards
    seq_len = shards * length
    table, table_low = tiled_table(seq_len, half)
    short_high, short_low = forward_table(2 * length, length)
    vmem = pl.BlockSpec(memory_space=pltpu.VMEM)
    half_type = jnp.bfloat16
    peers = pltpu.SemaphoreType.DMA((shards,))
    return pl.pallas_call(
        fused_kernel,
        out_shape=jax.ShapeDtypeStruct((channels, length), half_type),
        in_specs=[pl.BlockSpec(memory_space=pl.ANY)] * 9 + [vmem],
        out_specs=vmem,
        scratch_shapes=[
            pltpu.VMEM((channels, length), half_type),
            pltpu.VMEM((channels, length), half_type),
            pltpu.VMEM((channels, length), half_type),
            pltpu.VMEM((narrow, length), half_type),
            pltpu.VMEM((2 * length, 2 * length), half_type),
            pltpu.VMEM((2 * length, 2 * length), half_type),
            pltpu.VMEM((length, 2 * half), half_type),
            pltpu.VMEM((seq_len, 2 * half), half_type),
            pltpu.VMEM((channels, length), half_type),
            pltpu.VMEM((narrow, seq_len), half_type),
            pltpu.VMEM((narrow, seq_len), half_type),
            pltpu.VMEM((shards, narrow, length), half_type),
            pltpu.VMEM((shards, narrow, length), half_type),
            pltpu.VMEM((half // 128, narrow, 256), jnp.float32),
            pltpu.VMEM((narrow, 2 * half), half_type),
            pltpu.SemaphoreType.DMA((9,)),
            pltpu.SemaphoreType.DMA((2,)),
            peers, peers, peers, peers, peers, peers,
        ],
        compiler_params=pltpu.CompilerParams(
            collective_id=0, has_side_effects=True, vmem_limit_bytes=56 * 1024 * 1024
        ),
    )(features, gate_one, taps_one, long_filter, taps_two, short_high, short_low,
      table, table_low[:length], skip)


def exchange(blocks):
    return lax.all_to_all(blocks, RING, split_axis=0, concat_axis=0, tiled=True)


def on_device(features, gate_one, taps_one, long_filter, skip_gain, taps_two, gate_two):
    shards = lax.axis_size(RING)
    channels, block_len = features.shape
    narrow = channels // shards
    seq_len = block_len * shards
    length = taps_one.shape[1]

    first = lax.axis_index(RING) * narrow
    skip = lax.dynamic_slice_in_dim(skip_gain, first, narrow)[:, None]
    half = -(-(2 * seq_len + length) // 256) * 128
    if seq_len * half <= TABLE_LIMIT:
        second_conv = fused(
            features, gate_one, taps_one, long_filter, taps_two, skip, shards, half
        )
        return (second_conv.astype(jnp.float32) * gate_two).astype(jnp.bfloat16)

    def rows_of(blocks):
        return jnp.swapaxes(blocks, 0, 1).reshape(narrow, seq_len)

    filter_rows = rows_of(exchange(long_filter.reshape(shards, narrow, block_len)))
    before = lax.ppermute(features, RING, [(i, i + 1) for i in range(shards - 1)])
    mixed_one = (short_conv(before, features, taps_one) * gate_one).astype(jnp.bfloat16)
    signal = rows_of(exchange(mixed_one.reshape(shards, narrow, block_len)))
    taps = lax.dynamic_slice_in_dim(taps_two, first, narrow)
    result = factored_pair(signal, filter_rows, skip, taps)
    result = result.astype(jnp.bfloat16).reshape(narrow, shards, block_len)
    second_conv = exchange(jnp.swapaxes(result, 0, 1)).reshape(channels, block_len)
    return (second_conv.astype(jnp.float32) * gate_two).astype(jnp.bfloat16)


def solution(mesh):
    in_specs = (
        P("ch", ("grp", "tok", "sec")),
        P("ch", ("grp", "tok", "sec")),
        P("ch", None),
        P("ch", ("tok", "sec")),
        P("ch"),
        P("ch", None),
        P("ch", ("grp", "tok", "sec")),
    )
    out_specs = P("ch", ("grp", "tok", "sec"))
    return jax.shard_map(
        on_device, mesh=mesh, in_specs=in_specs, out_specs=out_specs, check_vma=False
    )
```

```python
import math

import jax
import jax.numpy as jnp
import ml_dtypes
import numpy as np
from jax import lax
from jax.experimental import pallas as pl
from jax.experimental.pallas import tpu as pltpu
from jax.sharding import PartitionSpec as P

RING = ("tok", "sec")
TABLE_LIMIT = 1 << 23


def angles(tokens, half):
    steps = (np.arange(tokens)[:, None] * (2 * np.arange(half)[None, :] + 1)) % (4 * half)
    return steps * (math.pi / (2 * half))


def two_pieces(table):
    high = table.astype(ml_dtypes.bfloat16)
    low = (table - high.astype(np.float64)).astype(ml_dtypes.bfloat16)
    return high, low


def forward_table(tokens, half):
    angle = angles(tokens, half)
    return two_pieces(np.concatenate([np.cos(angle), -np.sin(angle)], axis=1))


def backward_table(tokens, half):
    angle = angles(tokens, half).T
    return two_pieces(np.concatenate([np.cos(angle), -np.sin(angle)], axis=0) / half)


def dot(left, right):
    return jnp.dot(left, right, preferred_element_type=jnp.float32)


def forward(signal, table):
    return dot(signal, table[0]) + dot(signal, table[1])


def backward(spectrum, table):
    high = spectrum.astype(jnp.bfloat16)
    low = (spectrum - high.astype(jnp.float32)).astype(jnp.bfloat16)
    return dot(high, table[0]) + dot(low, table[0]) + dot(high, table[1])


def times(left, right):
    half = left.shape[1] // 2
    a, b = left[:, :half], left[:, half:]
    c, d = right[:, :half], right[:, half:]
    return jnp.concatenate([a * c - b * d, a * d + b * c], axis=1)


def short_conv(before, block, taps):
    length = taps.shape[1]
    table = forward_table(2 * length, length)
    back = backward_table(2 * length, length)
    early = tuple(piece[:length] for piece in table)
    late = tuple(piece[length:] for piece in table)
    spectrum = forward(before, early) + forward(block, late)
    product = times(spectrum, forward(taps, early))
    return backward(product, tuple(piece[:, length:] for piece in back))


def angle_table(rows_count, cols_count, period):
    row_index = jnp.arange(rows_count, dtype=jnp.int32)[:, None]
    col_index = jnp.arange(cols_count, dtype=jnp.int32)[None, :]
    phase = (row_index * col_index % period).astype(jnp.float32) * (2.0 * math.pi / period)
    return (jnp.cos(phase), jnp.sin(phase))


def contract(form, left, right):
    return jnp.einsum(form, left, right, precision=lax.Precision.HIGHEST)


def forward_spectrum(signal, outer, inner, total):
    half_outer = outer // 2
    cos_first, sin_first = angle_table(half_outer, outer, outer)
    turn_cos, turn_sin = angle_table(outer, inner, total)
    cos_inner, sin_inner = angle_table(inner, inner, inner)
    shaped = signal.reshape(signal.shape[0], half_outer, inner)
    real_a = contract("cmn,mk->ckn", shaped, cos_first)
    imag_a = -contract("cmn,mk->ckn", shaped, sin_first)
    real_b = real_a * turn_cos + imag_a * turn_sin
    imag_b = imag_a * turn_cos - real_a * turn_sin
    real_c = contract("ckn,nj->cjk", real_b, cos_inner) + contract("ckn,nj->cjk", imag_b, sin_inner)
    imag_c = contract("ckn,nj->cjk", imag_b, cos_inner) - contract("ckn,nj->cjk", real_b, sin_inner)
    return (real_c, imag_c)


def inverse_spectrum(real_y, imag_y, outer, inner, total):
    half_outer = outer // 2
    cos_inner, sin_inner = angle_table(inner, inner, inner)
    turn_cos, turn_sin = angle_table(outer, inner, total)
    cos_last, sin_last = angle_table(outer, half_outer, outer)
    real_c = contract("cjk,jn->ckn", real_y, cos_inner) - contract("cjk,jn->ckn", imag_y, sin_inner)
    imag_c = contract("cjk,jn->ckn", imag_y, cos_inner) + contract("cjk,jn->ckn", real_y, sin_inner)
    real_d = real_c * turn_cos - imag_c * turn_sin
    imag_d = imag_c * turn_cos + real_c * turn_sin
    result = contract("ckn,km->cmn", real_d, cos_last) - contract("ckn,km->cmn", imag_d, sin_last)
    return (result / total).reshape(real_y.shape[0], half_outer * inner)


def factored_pair(signal, filter_rows, skip, taps):
    channels, seq_len = signal.shape
    length = taps.shape[1]
    total = 2 * seq_len
    inner = math.gcd(seq_len, 128)
    outer = total // inner
    wide = signal.astype(jnp.float32)
    a, b = forward_spectrum(wide, outer, inner, total)
    c, d = forward_spectrum(filter_rows.astype(jnp.float32), outer, inner, total)
    rows = inverse_spectrum(a * c - b * d, a * d + b * c, outer, inner, total) + skip * wide
    rows = rows.astype(jnp.bfloat16)
    blocks = seq_len // length
    before = jnp.pad(rows, ((0, 0), (length, 0)))[:, :seq_len]
    result = short_conv(
        before.reshape(channels * blocks, length),
        rows.reshape(channels * blocks, length),
        jnp.repeat(taps, blocks, axis=0),
    )
    return result.reshape(channels, seq_len)


def tiled_table(tokens, half):
    angle = angles(tokens, half).reshape(tokens, half // 128, 1, 128)
    table = np.concatenate([np.cos(angle), -np.sin(angle)], axis=2)
    return two_pieces(table.reshape(tokens, 2 * half))


def dot_rows(left, right):
    return lax.dot_general(
        left, right, (((1,), (1,)), ((), ())), preferred_element_type=jnp.float32
    )


def split(wide):
    high = wide.astype(jnp.bfloat16)
    return high, (wide - high.astype(jnp.float32)).astype(jnp.bfloat16)


def fused_kernel(
    features_hbm, gate_hbm, taps_hbm, long_filter, taps_two, short_high_hbm, short_low_hbm,
    table_hbm, table_low_hbm, skip, second_conv,
    features, gate_one, taps_one, own_taps, short_high, short_low, table_low,
    table, before, filter_rows, signal, mixed_send, result_send, weights, high,
    load_sems, halo_sems, filter_sent, filter_got, mixed_sent, mixed_got, result_sent, result_got,
    relay_sent, relay_got,
):
    sections = lax.axis_size("sec")
    shards = lax.axis_size("tok") * sections
    me = lax.axis_index("tok") * sections + lax.axis_index("sec")
    narrow, seq_len = signal.shape
    length = features.shape[1]
    tiles = weights.shape[0]
    half = tiles * 128
    copies = lax.axis_size("grp")
    mine = lax.axis_index("grp")
    share = narrow // copies

    def share_rows(start, owner):
        return pl.ds(pl.multiple_of(start * narrow + owner * share, share), share)

    def place(peer):
        return {"tok": peer // sections, "sec": peer % sections}

    def rows(peer):
        return pl.ds(pl.multiple_of(peer * narrow, narrow), narrow)

    def tokens(peer):
        return pl.ds(pl.multiple_of(peer * length, length), length)

    def other(step):
        return lax.rem(me + step, shards)

    def remote(source, target, sent, got, peer):
        return pltpu.make_async_remote_copy(
            src_ref=source, dst_ref=target, send_sem=sent, recv_sem=got,
            device_id=place(peer), device_id_type=pl.DeviceIdType.MESH,
        )

    pairs = (
        (features_hbm, features), (taps_hbm, taps_one), (short_high_hbm, short_high),
        (short_low_hbm, short_low), (gate_hbm, gate_one),
        (long_filter.at[share_rows(me, mine)], filter_rows.at[share_rows(0, mine), tokens(me)]),
        (taps_two.at[rows(me)], own_taps), (table_low_hbm, table_low), (table_hbm, table),
    )
    loads = [
        pltpu.make_async_copy(source, target, load_sems.at[index])
        for index, (source, target) in enumerate(pairs)
    ]
    for load in loads:
        load.start()
    barrier = pltpu.get_barrier_semaphore()
    for step in range(1, shards):
        pl.semaphore_signal(
            barrier, inc=1, device_id=place(other(step)), device_id_type=pl.DeviceIdType.MESH
        )
    for step in range(1, copies):
        pl.semaphore_signal(
            barrier, inc=1, device_id={"grp": lax.rem(mine + step, copies)},
            device_id_type=pl.DeviceIdType.MESH,
        )
    pl.semaphore_wait(barrier, shards + copies - 2)

    halo = remote(features_hbm, before, halo_sems.at[0], halo_sems.at[1], other(1))

    @pl.when(me < shards - 1)
    def _():
        halo.start()

    def filter_copy(peer, slot):
        return remote(
            long_filter.at[share_rows(peer, mine)], filter_rows.at[share_rows(0, mine), tokens(slot)],
            filter_sent.at[peer], filter_got.at[slot], peer,
        )

    def relay_copy(peer, owner):
        part = filter_rows.at[share_rows(0, owner)]
        return pltpu.make_async_remote_copy(
            src_ref=part, dst_ref=part, send_sem=relay_sent.at[peer], recv_sem=relay_got.at[owner],
            device_id={"grp": peer}, device_id_type=pl.DeviceIdType.MESH,
        )

    def mixed_copy(peer, slot):
        return remote(
            mixed_send.at[peer], signal.at[:, tokens(slot)],
            mixed_sent.at[peer], mixed_got.at[slot], peer,
        )

    def result_copy(peer, slot):
        return remote(
            result_send.at[peer], second_conv.at[rows(slot)],
            result_sent.at[peer], result_got.at[slot], peer,
        )

    for step in range(1, shards):
        filter_copy(other(step), me).start()

    @pl.when(me == 0)
    def _():
        before[...] = jnp.zeros_like(before)

    @pl.when(me > 0)
    def _():
        halo.wait_recv()

    for load in loads[:5]:
        load.wait()
    early = (short_high[:length], short_low[:length])
    late = (short_high[length:], short_low[length:])

    def first_conv(peer):
        part = rows(peer)
        spectrum = forward(before[part], early) + forward(features[part], late)
        x_high, x_low = split(times(spectrum, forward(taps_one[part], early)))
        conv = dot_rows(x_high, late[0]) + dot_rows(x_low, late[0]) + dot_rows(x_high, late[1])
        return (conv * (1.0 / length) * gate_one[part].astype(jnp.float32)).astype(jnp.bfloat16)

    @pl.loop(1, shards)
    def _(step):
        peer = other(step)
        mixed_send[peer] = first_conv(peer)
        mixed_copy(peer, me).start()

    signal[:, tokens(me)] = first_conv(me)

    for load in loads[5:]:
        load.wait()
    for step in range(1, shards):
        filter_copy(other(step), other(step)).wait_recv()
    partners = [lax.rem(mine + step, copies) for step in range(1, copies)]
    for partner in partners:
        relay_copy(partner, mine).start()
    for partner in partners:
        relay_copy(partner, partner).wait_recv()

    def columns(tile):
        return pl.ds(pl.multiple_of(tile * 256, 256), 256)

    gain = skip[...]
    taps = own_taps[...]

    @pl.loop(0, tiles)
    def _(tile):
        own = columns(tile)
        spectrum = dot(filter_rows[...], table[:, own])
        spectrum = jnp.concatenate([spectrum[:, :128] + gain, spectrum[:, 128:]], axis=1)
        short = dot(taps, table[:length, own]) + dot(taps, table_low[:, own])
        weights[tile] = times(spectrum, short) * (1.0 / half)

    for step in range(1, shards):
        mixed_copy(other(step), other(step)).wait_recv()

    @pl.loop(0, tiles)
    def _(tile):
        own = columns(tile)
        product = times(dot(signal[...], table[:, own]), weights[tile])
        high[:, own] = product.astype(jnp.bfloat16)

    width = sections * length
    groups = shards // sections

    @pl.loop(1, groups + 1)
    def _(step):
        group = lax.rem(lax.axis_index("tok") + step, groups)
        part = table[pl.ds(pl.multiple_of(group * width, width), width)]
        result = dot_rows(high[...], part).astype(jnp.bfloat16)
        for section in range(sections):
            peer = group * sections + section
            block = result[:, section * length : (section + 1) * length]

            @pl.when(peer != me)
            def _():
                result_send[peer] = block
                result_copy(peer, me).start()

            @pl.when(peer == me)
            def _():
                second_conv[rows(me)] = block

    for step in range(1, shards):
        result_copy(other(step), other(step)).wait_recv()
    for step in range(1, shards):
        filter_copy(other(step), me).wait_send()
        mixed_copy(other(step), me).wait_send()
        result_copy(other(step), me).wait_send()
    for partner in partners:
        relay_copy(partner, mine).wait_send()

    @pl.when(me < shards - 1)
    def _():
        halo.wait_send()


def fused(features, gate_one, taps_one, long_filter, taps_two, skip, shards, half):
    copies = lax.axis_size("grp")
    channels, length = features.shape
    narrow = channels // shards
    seq_len = shards * length
    table, table_low = tiled_table(seq_len, half)
    short_high, short_low = forward_table(2 * length, length)
    vmem = pl.BlockSpec(memory_space=pltpu.VMEM)
    half_type = jnp.bfloat16
    peers = pltpu.SemaphoreType.DMA((shards,))
    return pl.pallas_call(
        fused_kernel,
        out_shape=jax.ShapeDtypeStruct((channels, length), half_type),
        in_specs=[pl.BlockSpec(memory_space=pl.ANY)] * 9 + [vmem],
        out_specs=vmem,
        scratch_shapes=[
            pltpu.VMEM((channels, length), half_type),
            pltpu.VMEM((channels, length), half_type),
            pltpu.VMEM((channels, length), half_type),
            pltpu.VMEM((narrow, length), half_type),
            pltpu.VMEM((2 * length, 2 * length), half_type),
            pltpu.VMEM((2 * length, 2 * length), half_type),
            pltpu.VMEM((length, 2 * half), half_type),
            pltpu.VMEM((seq_len, 2 * half), half_type),
            pltpu.VMEM((channels, length), half_type),
            pltpu.VMEM((narrow, seq_len), half_type),
            pltpu.VMEM((narrow, seq_len), half_type),
            pltpu.VMEM((shards, narrow, length), half_type),
            pltpu.VMEM((shards, narrow, length), half_type),
            pltpu.VMEM((half // 128, narrow, 256), jnp.float32),
            pltpu.VMEM((narrow, 2 * half), half_type),
            pltpu.SemaphoreType.DMA((9,)),
            pltpu.SemaphoreType.DMA((2,)),
            peers, peers, peers, peers, peers, peers,
            pltpu.SemaphoreType.DMA((copies,)), pltpu.SemaphoreType.DMA((copies,)),
        ],
        compiler_params=pltpu.CompilerParams(
            collective_id=0, has_side_effects=True, vmem_limit_bytes=56 * 1024 * 1024
        ),
    )(features, gate_one, taps_one, long_filter, taps_two, short_high, short_low,
      table, table_low[:length], skip)


def exchange(blocks):
    return lax.all_to_all(blocks, RING, split_axis=0, concat_axis=0, tiled=True)


def on_device(features, gate_one, taps_one, long_filter, skip_gain, taps_two, gate_two):
    shards = lax.axis_size(RING)
    channels, block_len = features.shape
    narrow = channels // shards
    seq_len = block_len * shards
    length = taps_one.shape[1]

    first = lax.axis_index(RING) * narrow
    skip = lax.dynamic_slice_in_dim(skip_gain, first, narrow)[:, None]
    half = -(-(2 * seq_len + length) // 256) * 128
    if seq_len * half <= TABLE_LIMIT:
        second_conv = fused(
            features, gate_one, taps_one, long_filter, taps_two, skip, shards, half
        )
        return (second_conv.astype(jnp.float32) * gate_two).astype(jnp.bfloat16)

    def rows_of(blocks):
        return jnp.swapaxes(blocks, 0, 1).reshape(narrow, seq_len)

    filter_rows = rows_of(exchange(long_filter.reshape(shards, narrow, block_len)))
    before = lax.ppermute(features, RING, [(i, i + 1) for i in range(shards - 1)])
    mixed_one = (short_conv(before, features, taps_one) * gate_one).astype(jnp.bfloat16)
    signal = rows_of(exchange(mixed_one.reshape(shards, narrow, block_len)))
    taps = lax.dynamic_slice_in_dim(taps_two, first, narrow)
    result = factored_pair(signal, filter_rows, skip, taps)
    result = result.astype(jnp.bfloat16).reshape(narrow, shards, block_len)
    second_conv = exchange(jnp.swapaxes(result, 0, 1)).reshape(channels, block_len)
    return (second_conv.astype(jnp.float32) * gate_two).astype(jnp.bfloat16)


def solution(mesh):
    in_specs = (
        P("ch", ("grp", "tok", "sec")),
        P("ch", ("grp", "tok", "sec")),
        P("ch", None),
        P("ch", ("tok", "sec")),
        P("ch"),
        P("ch", None),
        P("ch", ("grp", "tok", "sec")),
    )
    out_specs = P("ch", ("grp", "tok", "sec"))
    return jax.shard_map(
        on_device, mesh=mesh, in_specs=in_specs, out_specs=out_specs, check_vma=False
    )
```

```python
import math

import jax
import jax.numpy as jnp
import ml_dtypes
import numpy as np
from jax import lax
from jax.experimental import pallas as pl
from jax.experimental.pallas import tpu as pltpu
from jax.sharding import PartitionSpec as P

RING = ("tok", "sec")
TABLE_LIMIT = 1 << 23


def angles(tokens, half):
    steps = (np.arange(tokens)[:, None] * (2 * np.arange(half)[None, :] + 1)) % (4 * half)
    return steps * (math.pi / (2 * half))


def two_pieces(table):
    high = table.astype(ml_dtypes.bfloat16)
    low = (table - high.astype(np.float64)).astype(ml_dtypes.bfloat16)
    return high, low


def forward_table(tokens, half):
    angle = angles(tokens, half)
    return two_pieces(np.concatenate([np.cos(angle), -np.sin(angle)], axis=1))


def backward_table(tokens, half):
    angle = angles(tokens, half).T
    return two_pieces(np.concatenate([np.cos(angle), -np.sin(angle)], axis=0) / half)


def dot(left, right):
    return jnp.dot(left, right, preferred_element_type=jnp.float32)


def forward(signal, table):
    return dot(signal, table[0]) + dot(signal, table[1])


def backward(spectrum, table):
    high = spectrum.astype(jnp.bfloat16)
    low = (spectrum - high.astype(jnp.float32)).astype(jnp.bfloat16)
    return dot(high, table[0]) + dot(low, table[0]) + dot(high, table[1])


def times(left, right):
    half = left.shape[1] // 2
    a, b = left[:, :half], left[:, half:]
    c, d = right[:, :half], right[:, half:]
    return jnp.concatenate([a * c - b * d, a * d + b * c], axis=1)


def short_conv(before, block, taps):
    length = taps.shape[1]
    table = forward_table(2 * length, length)
    back = backward_table(2 * length, length)
    early = tuple(piece[:length] for piece in table)
    late = tuple(piece[length:] for piece in table)
    spectrum = forward(before, early) + forward(block, late)
    product = times(spectrum, forward(taps, early))
    return backward(product, tuple(piece[:, length:] for piece in back))


def angle_table(rows_count, cols_count, period):
    row_index = jnp.arange(rows_count, dtype=jnp.int32)[:, None]
    col_index = jnp.arange(cols_count, dtype=jnp.int32)[None, :]
    phase = (row_index * col_index % period).astype(jnp.float32) * (2.0 * math.pi / period)
    return (jnp.cos(phase), jnp.sin(phase))


def contract(form, left, right):
    return jnp.einsum(form, left, right, precision=lax.Precision.HIGHEST)


def forward_spectrum(signal, outer, inner, total):
    half_outer = outer // 2
    cos_first, sin_first = angle_table(half_outer, outer, outer)
    turn_cos, turn_sin = angle_table(outer, inner, total)
    cos_inner, sin_inner = angle_table(inner, inner, inner)
    shaped = signal.reshape(signal.shape[0], half_outer, inner)
    real_a = contract("cmn,mk->ckn", shaped, cos_first)
    imag_a = -contract("cmn,mk->ckn", shaped, sin_first)
    real_b = real_a * turn_cos + imag_a * turn_sin
    imag_b = imag_a * turn_cos - real_a * turn_sin
    real_c = contract("ckn,nj->cjk", real_b, cos_inner) + contract("ckn,nj->cjk", imag_b, sin_inner)
    imag_c = contract("ckn,nj->cjk", imag_b, cos_inner) - contract("ckn,nj->cjk", real_b, sin_inner)
    return (real_c, imag_c)


def inverse_spectrum(real_y, imag_y, outer, inner, total):
    half_outer = outer // 2
    cos_inner, sin_inner = angle_table(inner, inner, inner)
    turn_cos, turn_sin = angle_table(outer, inner, total)
    cos_last, sin_last = angle_table(outer, half_outer, outer)
    real_c = contract("cjk,jn->ckn", real_y, cos_inner) - contract("cjk,jn->ckn", imag_y, sin_inner)
    imag_c = contract("cjk,jn->ckn", imag_y, cos_inner) + contract("cjk,jn->ckn", real_y, sin_inner)
    real_d = real_c * turn_cos - imag_c * turn_sin
    imag_d = imag_c * turn_cos + real_c * turn_sin
    result = contract("ckn,km->cmn", real_d, cos_last) - contract("ckn,km->cmn", imag_d, sin_last)
    return (result / total).reshape(real_y.shape[0], half_outer * inner)


def factored_pair(signal, filter_rows, skip, taps):
    channels, seq_len = signal.shape
    length = taps.shape[1]
    total = 2 * seq_len
    inner = math.gcd(seq_len, 128)
    outer = total // inner
    wide = signal.astype(jnp.float32)
    a, b = forward_spectrum(wide, outer, inner, total)
    c, d = forward_spectrum(filter_rows.astype(jnp.float32), outer, inner, total)
    rows = inverse_spectrum(a * c - b * d, a * d + b * c, outer, inner, total) + skip * wide
    rows = rows.astype(jnp.bfloat16)
    blocks = seq_len // length
    before = jnp.pad(rows, ((0, 0), (length, 0)))[:, :seq_len]
    result = short_conv(
        before.reshape(channels * blocks, length),
        rows.reshape(channels * blocks, length),
        jnp.repeat(taps, blocks, axis=0),
    )
    return result.reshape(channels, seq_len)


def tiled_table(tokens, half):
    angle = angles(tokens, half).reshape(tokens, half // 128, 1, 128)
    table = np.concatenate([np.cos(angle), -np.sin(angle)], axis=2)
    return two_pieces(table.reshape(tokens, 2 * half))


def dot_rows(left, right):
    return lax.dot_general(
        left, right, (((1,), (1,)), ((), ())), preferred_element_type=jnp.float32
    )


def split(wide):
    high = wide.astype(jnp.bfloat16)
    return high, (wide - high.astype(jnp.float32)).astype(jnp.bfloat16)


def fused_kernel(
    features_hbm, gate_hbm, taps_hbm, long_filter, taps_two, short_high_hbm, short_low_hbm,
    table_hbm, table_low_hbm, skip, second_conv,
    features, gate_one, taps_one, own_taps, short_high, short_low, table_low,
    table, before, filter_rows, signal, mixed_send, result_send, weights, high,
    load_sems, halo_sems, filter_sent, filter_got, mixed_sent, mixed_got, result_sent, result_got,
    relay_sent, relay_got,
):
    sections = lax.axis_size("sec")
    shards = lax.axis_size("tok") * sections
    me = lax.axis_index("tok") * sections + lax.axis_index("sec")
    narrow, seq_len = signal.shape
    length = features.shape[1]
    tiles = weights.shape[0]
    half = tiles * 128
    copies = lax.axis_size("grp")
    mine = lax.axis_index("grp")
    share = narrow // copies

    def share_rows(start, owner):
        return pl.ds(pl.multiple_of(start * narrow + owner * share, share), share)

    def place(peer):
        return {"tok": peer // sections, "sec": peer % sections}

    def rows(peer):
        return pl.ds(pl.multiple_of(peer * narrow, narrow), narrow)

    def tokens(peer):
        return pl.ds(pl.multiple_of(peer * length, length), length)

    def other(step):
        return lax.rem(me + step, shards)

    def remote(source, target, sent, got, peer):
        return pltpu.make_async_remote_copy(
            src_ref=source, dst_ref=target, send_sem=sent, recv_sem=got,
            device_id=place(peer), device_id_type=pl.DeviceIdType.MESH,
        )

    pairs = (
        (features_hbm, features), (taps_hbm, taps_one), (short_high_hbm, short_high),
        (short_low_hbm, short_low), (gate_hbm, gate_one),
        (long_filter.at[share_rows(me, mine)], filter_rows.at[share_rows(0, mine), tokens(me)]),
        (taps_two.at[rows(me)], own_taps), (table_low_hbm, table_low), (table_hbm, table),
    )
    loads = [
        pltpu.make_async_copy(source, target, load_sems.at[index])
        for index, (source, target) in enumerate(pairs)
    ]
    for load in loads:
        load.start()
    barrier = pltpu.get_barrier_semaphore()
    for step in range(1, shards):
        pl.semaphore_signal(
            barrier, inc=1, device_id=place(other(step)), device_id_type=pl.DeviceIdType.MESH
        )
    for step in range(1, copies):
        pl.semaphore_signal(
            barrier, inc=1, device_id={"grp": lax.rem(mine + step, copies)},
            device_id_type=pl.DeviceIdType.MESH,
        )
    pl.semaphore_wait(barrier, shards + copies - 2)

    halo = remote(features_hbm, before, halo_sems.at[0], halo_sems.at[1], other(1))

    @pl.when(me < shards - 1)
    def _():
        halo.start()

    def filter_copy(peer, slot):
        return remote(
            long_filter.at[share_rows(peer, mine)], filter_rows.at[share_rows(0, mine), tokens(slot)],
            filter_sent.at[peer], filter_got.at[slot], peer,
        )

    def relay_copy(peer, owner):
        part = filter_rows.at[share_rows(0, owner)]
        return pltpu.make_async_remote_copy(
            src_ref=part, dst_ref=part, send_sem=relay_sent.at[peer], recv_sem=relay_got.at[owner],
            device_id={"grp": peer}, device_id_type=pl.DeviceIdType.MESH,
        )

    def mixed_copy(peer, slot):
        return remote(
            mixed_send.at[peer], signal.at[:, tokens(slot)],
            mixed_sent.at[peer], mixed_got.at[slot], peer,
        )

    def result_copy(peer, slot):
        return remote(
            result_send.at[peer], second_conv.at[rows(slot)],
            result_sent.at[peer], result_got.at[slot], peer,
        )


    @pl.when(me == 0)
    def _():
        before[...] = jnp.zeros_like(before)

    @pl.when(me > 0)
    def _():
        halo.wait_recv()

    for step in range(1, shards):
        filter_copy(other(step), me).start()

    for load in loads[:5]:
        load.wait()
    early = (short_high[:length], short_low[:length])
    late = (short_high[length:], short_low[length:])

    def first_conv(peer):
        part = rows(peer)
        spectrum = forward(before[part], early) + forward(features[part], late)
        x_high, x_low = split(times(spectrum, forward(taps_one[part], early)))
        conv = dot_rows(x_high, late[0]) + dot_rows(x_low, late[0]) + dot_rows(x_high, late[1])
        return (conv * (1.0 / length) * gate_one[part].astype(jnp.float32)).astype(jnp.bfloat16)

    @pl.loop(1, shards)
    def _(step):
        peer = other(step)
        mixed_send[peer] = first_conv(peer)
        mixed_copy(peer, me).start()

    signal[:, tokens(me)] = first_conv(me)

    for load in loads[5:]:
        load.wait()
    for step in range(1, shards):
        filter_copy(other(step), other(step)).wait_recv()
    partners = [lax.rem(mine + step, copies) for step in range(1, copies)]
    for partner in partners:
        relay_copy(partner, mine).start()
    for partner in partners:
        relay_copy(partner, partner).wait_recv()

    def columns(tile):
        return pl.ds(pl.multiple_of(tile * 256, 256), 256)

    gain = skip[...]
    taps = own_taps[...]

    @pl.loop(0, tiles)
    def _(tile):
        own = columns(tile)
        spectrum = dot(filter_rows[...], table[:, own])
        spectrum = jnp.concatenate([spectrum[:, :128] + gain, spectrum[:, 128:]], axis=1)
        short = dot(taps, table[:length, own]) + dot(taps, table_low[:, own])
        weights[tile] = times(spectrum, short) * (1.0 / half)

    for step in range(1, shards):
        mixed_copy(other(step), other(step)).wait_recv()

    @pl.loop(0, tiles)
    def _(tile):
        own = columns(tile)
        product = times(dot(signal[...], table[:, own]), weights[tile])
        high[:, own] = product.astype(jnp.bfloat16)

    width = sections * length
    groups = shards // sections

    @pl.loop(1, groups + 1)
    def _(step):
        group = lax.rem(lax.axis_index("tok") + step, groups)
        part = table[pl.ds(pl.multiple_of(group * width, width), width)]
        result = dot_rows(high[...], part).astype(jnp.bfloat16)
        for section in range(sections):
            peer = group * sections + section
            block = result[:, section * length : (section + 1) * length]

            @pl.when(peer != me)
            def _():
                result_send[peer] = block
                result_copy(peer, me).start()

            @pl.when(peer == me)
            def _():
                second_conv[rows(me)] = block

    for step in range(1, shards):
        result_copy(other(step), other(step)).wait_recv()
    for step in range(1, shards):
        filter_copy(other(step), me).wait_send()
        mixed_copy(other(step), me).wait_send()
        result_copy(other(step), me).wait_send()
    for partner in partners:
        relay_copy(partner, mine).wait_send()

    @pl.when(me < shards - 1)
    def _():
        halo.wait_send()


def fused(features, gate_one, taps_one, long_filter, taps_two, skip, shards, half):
    copies = lax.axis_size("grp")
    channels, length = features.shape
    narrow = channels // shards
    seq_len = shards * length
    table, table_low = tiled_table(seq_len, half)
    short_high, short_low = forward_table(2 * length, length)
    vmem = pl.BlockSpec(memory_space=pltpu.VMEM)
    half_type = jnp.bfloat16
    peers = pltpu.SemaphoreType.DMA((shards,))
    return pl.pallas_call(
        fused_kernel,
        out_shape=jax.ShapeDtypeStruct((channels, length), half_type),
        in_specs=[pl.BlockSpec(memory_space=pl.ANY)] * 9 + [vmem],
        out_specs=vmem,
        scratch_shapes=[
            pltpu.VMEM((channels, length), half_type),
            pltpu.VMEM((channels, length), half_type),
            pltpu.VMEM((channels, length), half_type),
            pltpu.VMEM((narrow, length), half_type),
            pltpu.VMEM((2 * length, 2 * length), half_type),
            pltpu.VMEM((2 * length, 2 * length), half_type),
            pltpu.VMEM((length, 2 * half), half_type),
            pltpu.VMEM((seq_len, 2 * half), half_type),
            pltpu.VMEM((channels, length), half_type),
            pltpu.VMEM((narrow, seq_len), half_type),
            pltpu.VMEM((narrow, seq_len), half_type),
            pltpu.VMEM((shards, narrow, length), half_type),
            pltpu.VMEM((shards, narrow, length), half_type),
            pltpu.VMEM((half // 128, narrow, 256), jnp.float32),
            pltpu.VMEM((narrow, 2 * half), half_type),
            pltpu.SemaphoreType.DMA((9,)),
            pltpu.SemaphoreType.DMA((2,)),
            peers, peers, peers, peers, peers, peers,
            pltpu.SemaphoreType.DMA((copies,)), pltpu.SemaphoreType.DMA((copies,)),
        ],
        compiler_params=pltpu.CompilerParams(
            collective_id=0, has_side_effects=True, vmem_limit_bytes=56 * 1024 * 1024
        ),
    )(features, gate_one, taps_one, long_filter, taps_two, short_high, short_low,
      table, table_low[:length], skip)


def exchange(blocks):
    return lax.all_to_all(blocks, RING, split_axis=0, concat_axis=0, tiled=True)


def on_device(features, gate_one, taps_one, long_filter, skip_gain, taps_two, gate_two):
    shards = lax.axis_size(RING)
    channels, block_len = features.shape
    narrow = channels // shards
    seq_len = block_len * shards
    length = taps_one.shape[1]

    first = lax.axis_index(RING) * narrow
    skip = lax.dynamic_slice_in_dim(skip_gain, first, narrow)[:, None]
    half = -(-(2 * seq_len + length) // 256) * 128
    if seq_len * half <= TABLE_LIMIT:
        second_conv = fused(
            features, gate_one, taps_one, long_filter, taps_two, skip, shards, half
        )
        return (second_conv.astype(jnp.float32) * gate_two).astype(jnp.bfloat16)

    def rows_of(blocks):
        return jnp.swapaxes(blocks, 0, 1).reshape(narrow, seq_len)

    filter_rows = rows_of(exchange(long_filter.reshape(shards, narrow, block_len)))
    before = lax.ppermute(features, RING, [(i, i + 1) for i in range(shards - 1)])
    mixed_one = (short_conv(before, features, taps_one) * gate_one).astype(jnp.bfloat16)
    signal = rows_of(exchange(mixed_one.reshape(shards, narrow, block_len)))
    taps = lax.dynamic_slice_in_dim(taps_two, first, narrow)
    result = factored_pair(signal, filter_rows, skip, taps)
    result = result.astype(jnp.bfloat16).reshape(narrow, shards, block_len)
    second_conv = exchange(jnp.swapaxes(result, 0, 1)).reshape(channels, block_len)
    return (second_conv.astype(jnp.float32) * gate_two).astype(jnp.bfloat16)


def solution(mesh):
    in_specs = (
        P("ch", ("grp", "tok", "sec")),
        P("ch", ("grp", "tok", "sec")),
        P("ch", None),
        P("ch", ("tok", "sec")),
        P("ch"),
        P("ch", None),
        P("ch", ("grp", "tok", "sec")),
    )
    out_specs = P("ch", ("grp", "tok", "sec"))
    return jax.shard_map(
        on_device, mesh=mesh, in_specs=in_specs, out_specs=out_specs, check_vma=False
    )
```
